128 devices in a mesh: gx: 16 (over y, z), gy: 8 (over x, core).
Axes of the slice: x: 4, y: 4, z: 4, core: 2. Of those that a mesh axis runs over, the one named last changes fastest.
Arguments:
- level_cotangent: float32 [256, 128, 128], P('gx', 'gy'), may hold values from -6 to 6
- velocity_cotangent: float32 [3, 256, 128, 128], P(None, 'gx', 'gy'), may hold values from -6 to 6
- fraction: float32 [2, 3, 256, 128, 128], P(None, None, 'gx', 'gy'), may hold values from 0 to 1
- shift_x: int32 [16, 8, 2], P('gx', 'gy'), may hold values from -2 to 2
- shift_y: int32 [16, 8, 2], P('gx', 'gy'), may hold values from -1 to 1
- region_labels: int32 [256, 128, 128], P('gx', 'gy'), may hold values 0 or 1
- phase_rates: float32 [2], replicated, may hold values from 0.04 to 0.16
Outputs:
- level_gradient: float32 [256, 128, 128], P('gx', 'gy')
- velocity_gradient: float32 [3, 256, 128, 128], P(None, 'gx', 'gy')
The draws below stay inside these ranges and needn't reach their ends.
All inputs are finite; a program needn't handle non-finite values. No bound on the sum of `region_labels` on one device may be relied on, other than what follows from the above.
Results may differ from the reference program's by a relative error of at most 0.0001.
Values sent between devices are 32-bit elements; how exact they have to be, the bound alone decides.
A program may use at most 128 MiB of HBM per device.

```python
import math
import jax
import jax.numpy as jnp

CX = 16
CY = 16
CZ = 128
STEPS = 2
TILES_X = 16
TILES_Y = 8
NX = 256
NY = 128


def set_ends(array, rng, low, high):
    place = [jax.random.randint(jax.random.fold_in(rng, axis), (), 0, length) for axis, length in enumerate(array.shape)]
    main_axis = array.shape.index(max(array.shape))
    beside = place[:main_axis] + [(place[main_axis] + 1) % array.shape[main_axis]] + place[main_axis + 1:]
    return array.at[tuple(place)].set(low).at[tuple(beside)].set(high)


def block_levels(own_key, shape, pieces, smallest, high):
    gain, own = 1.0, jax.random.fold_in(own_key, 6)
    for axis_at, blocks in pieces:
        steps = jnp.exp(jax.random.uniform(jax.random.fold_in(own, axis_at), (blocks,), jnp.float32, smallest / len(pieces), high / len(pieces)))
        gain = gain * jnp.repeat(steps, shape[axis_at] // blocks).reshape([-1 if axis == axis_at else 1 for axis in range(len(shape))])
    return gain


def scatter_about(rng, shape, deviation, most, pieces=(), kind=jnp.bfloat16):
    entries = deviation * jax.random.normal(rng, shape, jnp.float32)
    if pieces:
        entries = entries * block_levels(rng, shape, pieces, -0.22, 0.18)
    return jnp.clip(entries, -most, most).astype(kind)


def setup_inputs(seed: int = 0) -> dict:
    key_list = jax.random.split(jax.random.key(seed), 8)
    return {
        "level_cotangent": scatter_about(key_list[0], (NX, NY, CZ), 1.0, 6.0, ((0, 16), (1, 8)), jnp.float32),
        "velocity_cotangent": scatter_about(key_list[1], (3, NX, NY, CZ), 1.0, 6.0, ((1, 16), (2, 8)), jnp.float32),
        "fraction": jnp.clip(1.0 * jax.random.uniform(key_list[2], (STEPS, 3, NX, NY, CZ), jnp.float32) ** block_levels(key_list[2], (STEPS, 3, NX, NY, CZ), ((2, 16), (3, 8)), -0.2, 0.2), 0.0, 1.0),
        "shift_x": set_ends(jax.random.randint(key_list[3], (TILES_X, TILES_Y, STEPS), -2, 3), jax.random.fold_in(key_list[3], 1), -2, 2).astype(jnp.int32),
        "shift_y": set_ends(jax.random.randint(key_list[4], (TILES_X, TILES_Y, STEPS), -1, 2), jax.random.fold_in(key_list[4], 1), -1, 1).astype(jnp.int32),
        "region_labels": set_ends((jax.random.randint(key_list[5], (NX, NY, CZ), 0, 2) < 1).astype(jnp.int32), jax.random.fold_in(key_list[5], 1), 0, 1),
        "phase_rates": jnp.clip(jnp.exp(jax.random.uniform(key_list[6], (2,), jnp.float32, math.log(0.04), math.log(0.16))), 0.04, 0.16),
    }


BUOYANCY = 0.8


def cubic_weights(position):
    squared = position * position
    cubed = squared * position
    return ((2.0 * squared - cubed - position) * 0.5,
            (3.0 * cubed - 5.0 * squared + 2.0) * 0.5,
            (4.0 * squared - 3.0 * cubed + position) * 0.5,
            (cubed - squared) * 0.5)


def diffuse(values, cell_rate):
    summed = values
    for axis_index in (-3, -2, -1):
        for distance in (1, -1):
            neighbour = jnp.roll(values, distance, axis_index)
            neighbour_rate = jnp.roll(cell_rate, distance, axis_index)
            summed = summed + 0.5 * (cell_rate + neighbour_rate) * (neighbour - values)
    return summed


def to_tiles(values):
    lead_shape = values.shape[:-3]
    shaped = values.reshape(lead_shape + (TILES_X, CX, TILES_Y, CY, CZ))
    lead_count = len(lead_shape)
    axis_order = (lead_count, lead_count + 2) + tuple(range(lead_count)) + (lead_count + 1, lead_count + 3, lead_count + 4)
    return jnp.transpose(shaped, axis_order)


def spread_back(stacked, fractions, move_x, move_y):
    tiled = to_tiles(stacked)
    weights_x = cubic_weights(to_tiles(fractions[0]))
    weights_y = cubic_weights(to_tiles(fractions[1]))
    weights_z = cubic_weights(to_tiles(fractions[2]))
    patches = jnp.zeros((TILES_X, TILES_Y, 4, CX + 3, CY + 3, CZ), jnp.float32)
    for off_x in range(4):
        for off_y in range(4):
            weighted = tiled * (weights_x[off_x] * weights_y[off_y])[:, :, None]
            column = jnp.zeros_like(weighted)
            for off_z in range(4):
                column = column + jnp.roll(weighted * weights_z[off_z][:, :, None], off_z - 1, -1)
            patches = patches + jnp.pad(column, ((0, 0), (0, 0), (0, 0), (off_x, 3 - off_x), (off_y, 3 - off_y), (0, 0)))
    tile_x = jnp.arange(TILES_X, dtype=jnp.int32)[:, None]
    tile_y = jnp.arange(TILES_Y, dtype=jnp.int32)[None, :]
    target = ((tile_x + move_x.astype(jnp.int32)) % TILES_X) * TILES_Y + (tile_y + move_y.astype(jnp.int32)) % TILES_Y
    flat = patches.reshape((TILES_X * TILES_Y,) + patches.shape[2:])
    received = jax.ops.segment_sum(flat, target.reshape(-1).astype(jnp.int32), num_segments=TILES_X * TILES_Y).reshape(patches.shape)
    inner = received[:, :, :, 1:CX + 1]
    inner = inner.at[:, :, :, CX - 1:CX].add(jnp.roll(received[:, :, :, 0:1], -1, 0))
    inner = inner.at[:, :, :, 0:2].add(jnp.roll(received[:, :, :, CX + 1:CX + 3], 1, 0))
    folded = inner[:, :, :, :, 1:CY + 1]
    folded = folded.at[:, :, :, :, CY - 1:CY].add(jnp.roll(inner[:, :, :, :, 0:1], -1, 1))
    folded = folded.at[:, :, :, :, 0:2].add(jnp.roll(inner[:, :, :, :, CY + 1:CY + 3], 1, 1))
    return jnp.transpose(folded, (2, 0, 3, 1, 4, 5)).reshape(stacked.shape)


def reference(level_cotangent, velocity_cotangent, fraction, shift_x, shift_y, region_labels, phase_rates):
    cell_rate = jnp.where(region_labels == 1, phase_rates[1], phase_rates[0])
    level_now = level_cotangent
    velocity_now = velocity_cotangent
    for step_index in range(STEPS - 1, -1, -1):
        diffused = diffuse(diffuse(velocity_now, cell_rate), cell_rate)
        level_part = level_now + BUOYANCY * diffused[2]
        stacked = jnp.concatenate([level_part[None], diffused], 0)
        moved = spread_back(stacked, fraction[step_index], shift_x[:, :, step_index], shift_y[:, :, step_index])
        level_now = moved[0]
        velocity_now = moved[1:]
    return level_now, velocity_now
```

```python
import jax
import jax.numpy as jnp
from jax import lax
from jax.experimental import pallas as pl
from jax.experimental.pallas import tpu as pltpu
from jax.sharding import PartitionSpec as P

MESH = pl.DeviceIdType.MESH
BUOYANCY = 0.8
C = 16
Z = 128
ROW = (C, Z)
HALO = 24
PATCH = C + 3

PARTNERS = (
    [(d, 0) for d in (1, -1, 3, -3)]
    + [(0, d) for d in (1, -1, 2, -2)]
    + [(a, b) for a in (1, -1) for b in (1, -1)]
)


def cubic_weights(position):
    squared = position * position
    cubed = squared * position
    return (
        (2.0 * squared - cubed - position) * 0.5,
        (3.0 * cubed - 5.0 * squared + 2.0) * 0.5,
        (4.0 * squared - 3.0 * cubed + position) * 0.5,
        (cubed - squared) * 0.5,
    )


def rolled(value, shift, axis):
    shift = shift % value.shape[axis]
    return value if shift == 0 else pltpu.roll(value, shift, axis)


def make_kernel(count_x, count_y):
    def kernel(
        lev, vel, lab, frac_any, sx, sy, rates,
        out_l, out_v,
        frac, ext, mid, coef, dif, lvl, weight,
        to_up, to_down, to_rim, own, from_down, from_up, from_rim,
        edge_r, edge_l, tail_r, tail_l, got_tail_r, got_tail_l,
        got_r1, got_l1, next_r, next_l, got_r2, got_l2,
        send_sem, recv_sem, frac_sem,
    ):
        me_x = lax.axis_index("gx")
        me_y = lax.axis_index("gy")

        def partner(dx, dy):
            return (lax.rem(me_x + dx + count_x, count_x), lax.rem(me_y + dy + count_y, count_y))

        frac_copy = pltpu.make_async_copy(frac_any, frac, frac_sem)
        frac_copy.start()

        barrier = pltpu.get_barrier_semaphore()
        for dx, dy in PARTNERS:
            pl.semaphore_signal(barrier, inc=1, device_id=partner(dx, dy), device_id_type=MESH)

        started = []

        def send(src, dst, dx, dy):
            index = len(started)
            copy = pltpu.make_async_remote_copy(
                src_ref=src, dst_ref=dst, send_sem=send_sem.at[index], recv_sem=recv_sem.at[index],
                device_id=partner(dx, dy), device_id_type=MESH,
            )
            copy.start()
            started.append(copy)
            return copy

        for f in range(3):
            ext[0, f, 2 : C + 2, 0:C, :] = vel[f]
        ext[0, 3, 2 : C + 2, 0:C, :] = jnp.where(lab[...] == 1, rates[1], rates[0])
        pl.semaphore_wait(barrier, len(PARTNERS))

        def send_halo(step, fields):
            e = ext.at[step]
            lo, hi = C, C + 2
            f = pl.ds(0, fields)
            copies = [
                send(e.at[f, lo:hi, 0:C], e.at[f, 0:2, 0:C], 1, 0),
                send(e.at[f, 2:4, 0:C], e.at[f, hi : hi + 2, 0:C], -1, 0),
                send(e.at[f, 2:hi, C - 2 : C], e.at[f, 2:hi, HALO - 2 : HALO], 0, 1),
                send(e.at[f, 2:hi, 0:2], e.at[f, 2:hi, C : C + 2], 0, -1),
            ]
            for dx in (1, -1):
                for dy in (1, -1):
                    src_i, dst_i = (hi - 1, 1) if dx == 1 else (2, hi)
                    src_j, dst_j = (C - 1, HALO - 1) if dy == 1 else (0, C)
                    copies.append(
                        send(
                            e.at[f, src_i : src_i + 1, src_j : src_j + 1],
                            e.at[f, dst_i : dst_i + 1, dst_j : dst_j + 1],
                            dx, dy,
                        )
                    )
            return copies

        def coefficients():
            def body(i, carry):
                rate = ext[0, 3, i]
                k = [
                    0.5 * (rate + ext[0, 3, i + 1]),
                    0.5 * (rate + ext[0, 3, i - 1]),
                    0.5 * (rate + rolled(rate, -1, 0)),
                    0.5 * (rate + rolled(rate, 1, 0)),
                    0.5 * (rate + rolled(rate, -1, 1)),
                    0.5 * (rate + rolled(rate, 1, 1)),
                ]
                coef[0, i] = 1.0 - ((k[0] + k[1]) + (k[2] + k[3]) + (k[4] + k[5]))
                for n in range(6):
                    coef[n + 1, i] = k[n]
                return carry

            lax.fori_loop(1, C + 3, body, 0)

        def swept(src, f, i, height):
            v = src[f, i]
            low = slice(0, height)
            total = coef[0, i, low] * v[low]
            total += coef[1, i, low] * src[f, i + 1, low]
            total += coef[2, i, low] * src[f, i - 1, low]
            total += coef[3, i, low] * rolled(v, -1, 0)[low]
            total += coef[4, i, low] * rolled(v, 1, 0)[low]
            total += coef[5, i, low] * rolled(v[low], -1, 1)
            total += coef[6, i, low] * rolled(v[low], 1, 1)
            return total

        def diffuse(step):
            def first(i, carry):
                for f in range(3):
                    mid[f, i] = swept(ext.at[step], f, i, HALO)
                return carry

            lax.fori_loop(1, C + 3, first, 0)

            def second(i, carry):
                for f in range(3):
                    dif[f, i - 2] = swept(mid, f, i, C)
                return carry

            lax.fori_loop(2, C + 2, second, 0)

        def weights(step):
            def body(x, carry):
                for n, value in enumerate(cubic_weights(frac[step, 2, x])):
                    weight[n, x] = value
                for axis in range(2):
                    base = frac[step, axis, x]
                    for c in range(4):
                        for n, value in enumerate(cubic_weights(rolled(base, c - 1, 1))):
                            weight[4 + 16 * axis + 4 * c + n, x] = value
                return carry

            lax.fori_loop(0, C, body, 0)

        line = lax.broadcasted_iota(jnp.int32, ROW, 0)

        def spread(step, f, slot):
            row_y = jnp.full(ROW, sy[step], jnp.int32)
            up = jnp.where(row_y == 1, 1.0, 0.0)
            stay = jnp.where(row_y == 0, 1.0, 0.0)
            down = jnp.where(row_y == -1, 1.0, 0.0)
            high = line < C // 2
            stay_h = jnp.where(high, stay, 0.0)
            stay_l = jnp.where(high, 0.0, stay)
            rim_own = jnp.where(high, down, up)
            rim_far = jnp.where(high, up, down)

            def emit(r, main, rim):
                to_up[slot, r] = main * up + rim * stay_h
                to_down[slot, r] = main * down + rim * stay_l
                own[slot, r] = main * stay + rim * rim_own
                to_rim[slot, r] = rim * rim_far

            def body(x, carry):
                if f < 3:
                    g = dif[f, x]
                else:
                    g = lvl[x] + BUOYANCY * dif[2, x]
                sums = [[None] * 4 for _ in range(4)]
                for c in range(4):
                    gc = rolled(g * weight[c, x], c - 1, 1)
                    for b in range(4):
                        h = gc * weight[20 + 4 * c + b, x]
                        for a in range(4):
                            term = h * weight[4 + 4 * c + a, x]
                            sums[a][b] = term if c == 0 else sums[a][b] + term
                mains, rims = [], []
                for a in range(4):
                    below = rolled(sums[a][0], -1, 0)
                    above = rolled(sums[a][2], 1, 0)
                    above2 = rolled(sums[a][3], 2, 0)
                    mains.append(
                        sums[a][1]
                        + jnp.where(line == C - 1, 0.0, below)
                        + jnp.where(line == 0, 0.0, above)
                        + jnp.where(line < 2, 0.0, above2)
                    )
                    rims.append(
                        jnp.where(line == C - 1, below, 0.0)
                        + jnp.where(line == 0, above, 0.0)
                        + jnp.where(line < 2, above2, 0.0)
                    )
                m0, m1, m2, r0, r1, r2 = carry
                emit(x, m0 + mains[0], r0 + rims[0])
                return (m1 + mains[1], m2 + mains[2], mains[3], r1 + rims[1], r2 + rims[2], rims[3])

            zero = jnp.zeros(ROW, jnp.float32)
            m0, m1, m2, r0, r1, r2 = lax.fori_loop(0, C, body, (zero,) * 6)
            emit(C, m0, r0)
            emit(C + 1, m1, r1)
            emit(C + 2, m2, r2)
            meta = jnp.full(ROW, sx[step], jnp.int32).astype(jnp.float32)
            to_up[slot, PATCH] = meta
            to_down[slot, PATCH] = meta
            to_rim[slot, PATCH] = meta
            own[slot, PATCH] = meta
            return [
                send(to_up.at[slot], from_down.at[slot], 0, 1),
                send(to_down.at[slot], from_up.at[slot], 0, -1),
                send(to_rim.at[slot, :, 0:2], from_rim.at[slot, :, 0:2], 0, 2),
                send(to_rim.at[slot, :, C - 1 : C], from_rim.at[slot, :, C - 1 : C], 0, -2),
            ]

        sources = (own, from_down, from_up, from_rim)
        rim_lines = (line < 2) | (line == C - 1)

        def masks(slot, move):
            found = []
            for n, source in enumerate(sources):
                hit = source[slot, PATCH] == float(move)
                found.append(hit & rim_lines if n == 3 else hit)
            return found

        def gathered(slot, hits, r):
            total = None
            for hit, source in zip(hits, sources):
                part = jnp.where(hit, source[slot, r], 0.0)
                total = part if total is None else total + part
            return total

        def build(slot, move, store, load_extra=None):
            hits = masks(slot, move)
            before = masks(slot, move - 1) if move > -2 else None
            after = masks(slot, move + 1) if move < 2 else None

            def row(q, extra_sum):
                total = gathered(slot, hits, q + 1)
                if load_extra is not None:
                    total = total + load_extra(q)
                if extra_sum is not None:
                    total = total + extra_sum
                store(q, total)

            def body(q, carry):
                row(q, None)
                return carry

            first = 2 if before is not None else 0
            last = C - 1 if after is not None else C
            if before is not None:
                row(0, gathered(slot, before, C + 1))
                row(1, gathered(slot, before, C + 2))
            lax.fori_loop(first, last, body, 0)
            if after is not None:
                row(C - 1, gathered(slot, after, 0))

        def store_to(ref, slot):
            def store(q, value):
                ref[slot, q] = value

            return store

        def outer(slot):
            build(slot, 2, store_to(edge_r, slot))
            copies = [send(edge_r.at[slot], got_r1.at[slot], 1, 0)]
            build(slot, -2, store_to(edge_l, slot))
            copies.append(send(edge_l.at[slot], got_l1.at[slot], -1, 0))
            hits = masks(slot, 2)
            tail_r[slot, 0] = gathered(slot, hits, C + 1)
            tail_r[slot, 1] = gathered(slot, hits, C + 2)
            tail_l[slot, 0] = gathered(slot, masks(slot, -2), 0)
            copies.append(send(tail_r.at[slot], got_tail_r.at[slot], 3, 0))
            copies.append(send(tail_l.at[slot], got_tail_l.at[slot], -3, 0))
            return copies

        def inner(slot, copies):
            copies[0].wait_recv()
            build(slot, 1, store_to(next_r, slot), lambda q: got_r1[slot, q])
            right = send(next_r.at[slot], got_r2.at[slot], 1, 0)
            copies[1].wait_recv()
            build(slot, -1, store_to(next_l, slot), lambda q: got_l1[slot, q])
            left = send(next_l.at[slot], got_l2.at[slot], -1, 0)
            return [right, left, copies[2], copies[3]]

        def finish(slot, copies, load, store):
            for copy in copies:
                copy.wait_recv()
            build(slot, 0, store, lambda q: got_r2[slot, q] + got_l2[slot, q])
            store(0, load(0) + got_tail_r[slot, 0])
            store(1, load(1) + got_tail_r[slot, 1])
            store(C - 1, load(C - 1) + got_tail_l[slot, 0])

        def target(step, f):
            if step == 0 and f < 3:
                def store(q, value):
                    ext[1, f, q + 2, 0:C] = value

                def load(q):
                    return ext[1, f, q + 2, 0:C]
            elif step == 0:
                def store(q, value):
                    lvl[q] = value

                def load(q):
                    return lvl[q]
            elif f < 3:
                def store(q, value):
                    out_v[f, q] = value

                def load(q):
                    return out_v[f, q]
            else:
                def store(q, value):
                    out_l[q] = value

                def load(q):
                    return out_l[q]
            return load, store

        def wait_all(copies):
            for copy in copies:
                copy.wait_recv()

        halo = send_halo(0, 4)
        lvl[...] = lev[...]
        frac_copy.wait()
        weights(1)
        pending = None
        for step in range(2):
            when = 1 - step
            base = 4 * step
            wait_all(halo)
            if step == 0:
                coefficients()
            diffuse(step)
            chain = [None] * 4
            passed = [None] * 4
            passed[0] = spread(when, 0, base)
            passed[1] = spread(when, 1, base + 1)
            wait_all(passed[0])
            chain[0] = outer(base)
            passed[2] = spread(when, 2, base + 2)
            wait_all(passed[1])
            chain[1] = outer(base + 1)
            if step == 1:
                finish(base - 1, pending, *target(0, 3))
            passed[3] = spread(when, 3, base + 3)
            wait_all(passed[2])
            chain[2] = outer(base + 2)
            for f in range(3):
                chain[f] = inner(base + f, chain[f])
            wait_all(passed[3])
            chain[3] = outer(base + 3)
            if step == 0:
                weights(0)
            for f in range(3):
                finish(base + f, chain[f], *target(step, f))
            if step == 0:
                halo = send_halo(1, 3)
            pending = inner(base + 3, chain[3])
        finish(7, pending, *target(1, 3))
        for copy in started:
            copy.wait_send()

    return kernel


def solution(mesh):
    count_x, count_y = mesh.shape["gx"], mesh.shape["gy"]
    copies = 2 * (8 + 4 * 10)

    def on_device(level, velocity, fraction, shift_x, shift_y, labels, rates):
        vmem = pl.BlockSpec(memory_space=pltpu.VMEM)
        smem = pl.BlockSpec(memory_space=pltpu.SMEM)
        f32 = jnp.float32

        def rows(*lead):
            return pltpu.VMEM(lead + ROW, f32)

        return pl.pallas_call(
            make_kernel(count_x, count_y),
            name="adjoint",
            out_shape=(
                jax.ShapeDtypeStruct((C, C, Z), f32),
                jax.ShapeDtypeStruct((3, C, C, Z), f32),
            ),
            in_specs=[vmem, vmem, vmem, pl.BlockSpec(memory_space=pl.ANY), smem, smem, smem],
            out_specs=(vmem, vmem),
            scratch_shapes=[
                rows(2, 3, C),
                pltpu.VMEM((2, 4, C + 4, HALO, Z), f32),
                pltpu.VMEM((3, C + 4, HALO, Z), f32),
                pltpu.VMEM((7, C + 4, HALO, Z), f32),
                rows(3, C),
                rows(C),
                rows(36, C),
                rows(8, PATCH + 1), rows(8, PATCH + 1), rows(8, PATCH + 1), rows(8, PATCH + 1),
                rows(8, PATCH + 1), rows(8, PATCH + 1), rows(8, PATCH + 1),
                rows(8, C), rows(8, C), rows(8, 2), rows(8, 1), rows(8, 2), rows(8, 1),
                rows(8, C), rows(8, C), rows(8, C), rows(8, C), rows(8, C), rows(8, C),
                pltpu.SemaphoreType.DMA((copies,)),
                pltpu.SemaphoreType.DMA((copies,)),
                pltpu.SemaphoreType.DMA,
            ],
            compiler_params=pltpu.CompilerParams(
                collective_id=0, has_side_effects=True, vmem_limit_bytes=56 * 2**20
            ),
        )(level, velocity, labels, fraction, shift_x.reshape(2), shift_y.reshape(2), rates)

    field = P("gx", "gy", None)
    stack = P(None, "gx", "gy", None)
    return jax.shard_map(
        on_device,
        mesh=mesh,
        in_specs=(field, stack, P(None, None, "gx", "gy", None), field, field, field, P()),
        out_specs=(field, stack),
        check_vma=False,
    )
```

```python
import jax
import jax.numpy as jnp
from jax import lax
from jax.experimental import pallas as pl
from jax.experimental.pallas import tpu as pltpu
from jax.sharding import PartitionSpec as P

MESH = pl.DeviceIdType.MESH
BUOYANCY = 0.8
C = 16
Z = 128
ROW = (C, Z)
HALO = 24
PATCH = C + 3
U_COEF, U_FIRST, U_SECOND, U_WEIGHT, U_SPREAD, U_BUILD = 3, 6, 4, 2, 2, 7
ORDER = (
    "d02", "s02", "d00", "s00", "g02", "d01", "s01", "g00", "s03", "c02", "c00", "g01",
    "f02", "f00", "g03", "c01", "d12", "s12", "c03", "d10", "s10", "f01", "g12", "f03",
    "s13", "g10", "c12", "d11", "s11", "c10", "g13", "f12", "g11", "c13", "f10", "c11",
    "f13", "f11",
)
PARTS = 1

PARTNERS = (
    [(d, 0) for d in (1, -1, 3, -3)]
    + [(0, d) for d in (1, -1, 2, -2)]
    + [(a, b) for a in (1, -1) for b in (1, -1)]
)


def cubic_weights(position):
    squared = position * position
    cubed = squared * position
    return (
        (2.0 * squared - cubed - position) * 0.5,
        (3.0 * cubed - 5.0 * squared + 2.0) * 0.5,
        (4.0 * squared - 3.0 * cubed + position) * 0.5,
        (cubed - squared) * 0.5,
    )


def rolled(value, shift, axis):
    shift = shift % value.shape[axis]
    return value if shift == 0 else pltpu.roll(value, shift, axis)


def loop(low, high, body, carry, width):
    whole = (high - low) // width

    def several(n, carry):
        for k in range(width):
            carry = body(low + n * width + k, carry)
        return carry

    if whole > 1:
        carry = lax.fori_loop(0, whole, several, carry)
    else:
        whole = 0
    for i in range(low + whole * width, high):
        carry = body(i, carry)
    return carry


def make_kernel(count_x, count_y):
    def kernel(
        lev_any, vel_any, lab_any, frac_any, sx, sy, rates,
        out_l, out_v,
        frac, lab, ext, mid, coef, dif, lvl, weight,
        to_up, to_down, to_rim, own, from_down, from_up, from_rim,
        tail_r, tail_l, got_tail_r, got_tail_l,
        far_r, far_l, near_r, near_l, got_far_r, got_far_l, got_near_r, got_near_l,
        send_sem, recv_sem, load_sem,
    ):
        me_x = lax.axis_index("gx")
        me_y = lax.axis_index("gy")

        def partner(dx, dy):
            return (lax.rem(me_x + dx + count_x, count_x), lax.rem(me_y + dy + count_y, count_y))

        barrier = pltpu.get_barrier_semaphore()
        for dx, dy in PARTNERS:
            pl.semaphore_signal(barrier, inc=1, device_id=partner(dx, dy), device_id_type=MESH)

        inner = ext.at[0, 0:3, 2 : C + 2, 0:C]
        loads = [
            pltpu.make_async_copy(src, dst, load_sem.at[n])
            for n, (src, dst) in enumerate(((lab_any, lab), (vel_any, inner), (frac_any, frac), (lev_any, lvl)))
        ]
        for load in loads:
            load.start()

        started = []

        def send(src, dst, dx, dy):
            index = len(started)
            copy = pltpu.make_async_remote_copy(
                src_ref=src, dst_ref=dst, send_sem=send_sem.at[index], recv_sem=recv_sem.at[index],
                device_id=partner(dx, dy), device_id_type=MESH,
            )
            copy.start()
            started.append(copy)
            return copy

        loads[0].wait()
        ext[0, 3, 2 : C + 2, 0:C, :] = jnp.where(lab[...] == 1, rates[1], rates[0])
        loads[1].wait()
        pl.semaphore_wait(barrier, len(PARTNERS))

        def send_halo(step, first, fields):
            e = ext.at[step]
            lo, hi = C, C + 2
            f = pl.ds(first, fields)
            copies = [
                send(e.at[f, lo:hi, 0:C], e.at[f, 0:2, 0:C], 1, 0),
                send(e.at[f, 2:4, 0:C], e.at[f, hi : hi + 2, 0:C], -1, 0),
                send(e.at[f, 2:hi, C - 2 : C], e.at[f, 2:hi, HALO - 2 : HALO], 0, 1),
                send(e.at[f, 2:hi, 0:2], e.at[f, 2:hi, C : C + 2], 0, -1),
            ]
            for dx in (1, -1):
                for dy in (1, -1):
                    src_i, dst_i = (hi - 1, 1) if dx == 1 else (2, hi)
                    src_j, dst_j = (C - 1, HALO - 1) if dy == 1 else (0, C)
                    copies.append(
                        send(
                            e.at[f, src_i : src_i + 1, src_j : src_j + 1],
                            e.at[f, dst_i : dst_i + 1, dst_j : dst_j + 1],
                            dx, dy,
                        )
                    )
            return copies

        def coefficients():
            def body(i, carry):
                rate = ext[0, 3, i]
                k = [
                    0.5 * (rate + ext[0, 3, i + 1]),
                    0.5 * (rate + ext[0, 3, i - 1]),
                    0.5 * (rate + rolled(rate, -1, 0)),
                    0.5 * (rate + rolled(rate, 1, 0)),
                    0.5 * (rate + rolled(rate, -1, 1)),
                    0.5 * (rate + rolled(rate, 1, 1)),
                ]
                coef[0, i] = 1.0 - ((k[0] + k[1]) + (k[2] + k[3]) + (k[4] + k[5]))
                for n in range(6):
                    coef[n + 1, i] = k[n]
                return carry

            loop(1, C + 3, body, 0, U_COEF)

        def swept(src, f, i, height):
            v = src[f, i]
            low = slice(0, height)
            total = coef[0, i, low] * v[low]
            total += coef[1, i, low] * src[f, i + 1, low]
            total += coef[2, i, low] * src[f, i - 1, low]
            total += coef[3, i, low] * rolled(v, -1, 0)[low]
            total += coef[4, i, low] * rolled(v, 1, 0)[low]
            total += coef[5, i, low] * rolled(v[low], -1, 1)
            total += coef[6, i, low] * rolled(v[low], 1, 1)
            return total

        def diffuse(step, f):
            def first(i, carry):
                mid[f, i] = swept(ext.at[step], f, i, HALO)
                return carry

            loop(1, C + 3, first, 0, U_FIRST)

            def second(i, carry):
                dif[f, i - 2] = swept(mid, f, i, C)
                return carry

            loop(2, C + 2, second, 0, U_SECOND)

        def weights(step):
            def body(x, carry):
                for n, value in enumerate(cubic_weights(frac[step, 2, x])):
                    weight[step, n, x] = value
                for axis in range(2):
                    base = frac[step, axis, x]
                    for c in range(4):
                        for n, value in enumerate(cubic_weights(rolled(base, c - 1, 1))):
                            weight[step, 4 + 16 * axis + 4 * c + n, x] = value
                return carry

            loop(0, C, body, 0, U_WEIGHT)

        line = lax.broadcasted_iota(jnp.int32, ROW, 0)

        def spread(step, f, slot):
            row_y = jnp.full(ROW, sy[step], jnp.int32)
            up = jnp.where(row_y == 1, 1.0, 0.0)
            stay = jnp.where(row_y == 0, 1.0, 0.0)
            down = jnp.where(row_y == -1, 1.0, 0.0)
            high = line < C // 2
            stay_h = jnp.where(high, stay, 0.0)
            stay_l = jnp.where(high, 0.0, stay)
            rim_own = jnp.where(high, down, up)
            rim_far = jnp.where(high, up, down)

            def emit(r, main, rim):
                to_up[slot, r] = main * up + rim * stay_h
                to_down[slot, r] = main * down + rim * stay_l
                own[slot, r] = main * stay + rim * rim_own
                to_rim[slot, r] = rim * rim_far

            def body(x, carry):
                if f < 3:
                    g = dif[f, x]
                else:
                    g = lvl[x] + BUOYANCY * dif[2, x]
                sums = [[None] * 4 for _ in range(4)]
                for c in range(4):
                    gc = rolled(g * weight[step, c, x], c - 1, 1)
                    for b in range(4):
                        h = gc * weight[step, 20 + 4 * c + b, x]
                        for a in range(4):
                            term = h * weight[step, 4 + 4 * c + a, x]
                            sums[a][b] = term if c == 0 else sums[a][b] + term
                mains, rims = [], []
                for a in range(4):
                    below = rolled(sums[a][0], -1, 0)
                    above = rolled(sums[a][2], 1, 0)
                    above2 = rolled(sums[a][3], 2, 0)
                    mains.append(
                        sums[a][1]
                        + jnp.where(line == C - 1, 0.0, below)
                        + jnp.where(line == 0, 0.0, above)
                        + jnp.where(line < 2, 0.0, above2)
                    )
                    rims.append(
                        jnp.where(line == C - 1, below, 0.0)
                        + jnp.where(line == 0, above, 0.0)
                        + jnp.where(line < 2, above2, 0.0)
                    )
                m0, m1, m2, r0, r1, r2 = carry
                emit(x, m0 + mains[0], r0 + rims[0])
                return (m1 + mains[1], m2 + mains[2], mains[3], r1 + rims[1], r2 + rims[2], rims[3])

            zero = jnp.zeros(ROW, jnp.float32)
            half = C // 2
            early, late = pl.ds(0, half), pl.ds(half, PATCH + 1 - half)
            carry = loop(0, half, body, (zero,) * 6, U_SPREAD)
            copies = [
                send(to_up.at[slot, early], from_down.at[slot, early], 0, 1),
                send(to_down.at[slot, early], from_up.at[slot, early], 0, -1),
            ]
            m0, m1, m2, r0, r1, r2 = loop(half, C, body, carry, U_SPREAD)
            emit(C, m0, r0)
            emit(C + 1, m1, r1)
            emit(C + 2, m2, r2)
            meta = jnp.full(ROW, sx[step], jnp.int32).astype(jnp.float32)
            to_up[slot, PATCH] = meta
            to_down[slot, PATCH] = meta
            to_rim[slot, PATCH] = meta
            own[slot, PATCH] = meta
            return copies + [
                send(to_up.at[slot, late], from_down.at[slot, late], 0, 1),
                send(to_down.at[slot, late], from_up.at[slot, late], 0, -1),
                send(to_rim.at[slot, :, 0:2], from_rim.at[slot, :, 0:2], 0, 2),
                send(to_rim.at[slot, :, C - 1 : C], from_rim.at[slot, :, C - 1 : C], 0, -2),
            ]

        sources = (own, from_down, from_up, from_rim)
        rim_lines = (line < 2) | (line == C - 1)

        def masks(slot, move):
            found = []
            wanted = jnp.full(ROW, move, jnp.int32).astype(jnp.float32)
            for n, source in enumerate(sources):
                hit = source[slot, PATCH] == wanted
                found.append(hit & rim_lines if n == 3 else hit)
            return found

        def gathered(slot, hits, r):
            total = None
            for hit, source in zip(hits, sources):
                part = jnp.where(hit, source[slot, r], 0.0)
                total = part if total is None else total + part
            return total

        def build(slot, move, low, high, store, load_extra=None):
            hits = masks(slot, move)

            def row(q, rim):
                total = gathered(slot, hits, q + 1)
                if load_extra is not None:
                    total = total + load_extra(q)
                if rim is not None:
                    total = total + rim
                store(q, total)

            def body(q, carry):
                row(q, None)
                return carry

            first, last = low, high
            if low == 0:
                before = masks(slot, move - 1)
                row(0, gathered(slot, before, C + 1))
                row(1, gathered(slot, before, C + 2))
                first = 2
            if high == C:
                last = C - 1
            loop(first, last, body, 0, U_BUILD)
            if high == C:
                row(C - 1, gathered(slot, masks(slot, move + 1), 0))

        def parts():
            size = C // PARTS
            return [(n * size, n * size + size) for n in range(PARTS)]

        def transfer(slot, move, src, dst, dx, arrivals=None, arrived=None):
            copies = []
            for n, (low, high) in enumerate(parts()):
                if arrivals is not None:
                    arrivals[n].wait_recv()

                def store(q, value):
                    src[slot, q] = value

                build(slot, move, low, high, store, None if arrived is None else lambda q: arrived[slot, q])
                rows = pl.ds(low, high - low)
                copies.append(send(src.at[slot, rows], dst.at[slot, rows], dx, 0))
            return copies

        def outer(slot):
            right = transfer(slot, 2, far_r, got_far_r, 1)
            left = transfer(slot, -2, far_l, got_far_l, -1)
            hits = masks(slot, 2)
            tail_r[slot, 0] = gathered(slot, hits, C + 1)
            tail_r[slot, 1] = gathered(slot, hits, C + 2)
            tail_l[slot, 0] = gathered(slot, masks(slot, -2), 0)
            tails = [
                send(tail_r.at[slot], got_tail_r.at[slot], 3, 0),
                send(tail_l.at[slot], got_tail_l.at[slot], -3, 0),
            ]
            return right, left, tails

        def finish(slot, copies, load, store):
            wait_all(copies)
            build(slot, 0, 0, C, store, lambda q: got_near_r[slot, q] + got_near_l[slot, q])
            store(0, load(0) + got_tail_r[slot, 0])
            store(1, load(1) + got_tail_r[slot, 1])
            store(C - 1, load(C - 1) + got_tail_l[slot, 0])

        def target(step, f):
            if step == 0 and f < 3:
                def store(q, value):
                    ext[1, f, q + 2, 0:C] = value

                def load(q):
                    return ext[1, f, q + 2, 0:C]
            elif step == 0:
                def store(q, value):
                    lvl[q] = value

                def load(q):
                    return lvl[q]
            elif f < 3:
                def store(q, value):
                    out_v[f, q] = value

                def load(q):
                    return out_v[f, q]
            else:
                def store(q, value):
                    out_l[q] = value

                def load(q):
                    return out_l[q]
            return load, store

        def wait_all(copies):
            for copy in copies:
                copy.wait_recv()

        halo = {(0, f): [] for f in range(3)}
        halo[0, 2] = send_halo(0, 0, 4)
        loads[2].wait()
        loads[3].wait()
        weights(1)
        weights(0)
        state = {}

        def do_d(step, f):
            wait_all(halo[step, f])
            if (step, f) == (0, 2):
                coefficients()
            diffuse(step, f)

        def do_s(step, f):
            state[step, f] = spread(1 - step, f, 4 * step + f)

        def do_g(step, f):
            wait_all(state[step, f])
            state[step, f] = outer(4 * step + f)

        def do_c(step, f):
            right, left, rest = state[step, f]
            slot = 4 * step + f
            right = transfer(slot, 1, near_r, got_near_r, 1, right, got_far_r)
            left = transfer(slot, -1, near_l, got_near_l, -1, left, got_far_l)
            state[step, f] = right + left + rest

        def do_f(step, f):
            finish(4 * step + f, state[step, f], *target(step, f))
            if step == 0 and f < 3:
                halo[1, f] = send_halo(1, f, 1)

        todo = {"d": do_d, "s": do_s, "g": do_g, "c": do_c, "f": do_f}
        for word in ORDER:
            todo[word[0]](int(word[1]), int(word[2]))
        for copy in started:
            copy.wait_send()

    return kernel


def solution(mesh):
    count_x, count_y = mesh.shape["gx"], mesh.shape["gy"]
    copies = 8 + 3 * 8 + 2 * 4 * (6 + 2 + 4 * PARTS)

    def on_device(level, velocity, fraction, shift_x, shift_y, labels, rates):
        vmem = pl.BlockSpec(memory_space=pltpu.VMEM)
        smem = pl.BlockSpec(memory_space=pltpu.SMEM)
        f32 = jnp.float32

        def rows(*lead):
            return pltpu.VMEM(lead + ROW, f32)

        level_out, velocity_out = pl.pallas_call(
            make_kernel(count_x, count_y),
            name="adjoint",
            out_shape=(
                jax.ShapeDtypeStruct((C, C, Z), f32),
                jax.ShapeDtypeStruct((3, C, C, Z), f32),
            ),
            in_specs=[pl.BlockSpec(memory_space=pl.ANY)] * 4 + [smem] * 3,
            out_specs=(vmem, vmem),
            scratch_shapes=[
                rows(2, 3, C),
                pltpu.VMEM((C, C, Z), jnp.int32),
                pltpu.VMEM((2, 4, C + 4, HALO, Z), f32),
                pltpu.VMEM((3, C + 4, HALO, Z), f32),
                pltpu.VMEM((7, C + 4, HALO, Z), f32),
                rows(3, C),
                rows(C),
                rows(2, 36, C),
                rows(8, PATCH + 1), rows(8, PATCH + 1), rows(8, PATCH + 1), rows(8, PATCH + 1),
                rows(8, PATCH + 1), rows(8, PATCH + 1), rows(8, PATCH + 1),
                rows(8, 2), rows(8, 1), rows(8, 2), rows(8, 1),
                rows(8, C), rows(8, C), rows(8, C), rows(8, C), rows(8, C), rows(8, C), rows(8, C), rows(8, C),
                pltpu.SemaphoreType.DMA((copies,)),
                pltpu.SemaphoreType.DMA((copies,)),
                pltpu.SemaphoreType.DMA((4,)),
            ],
            compiler_params=pltpu.CompilerParams(
                collective_id=0, has_side_effects=True, vmem_limit_bytes=56 * 2**20
            ),
        )(level, velocity, labels, fraction, shift_x.reshape(2), shift_y.reshape(2), rates)

        def hand_over(a, b, to_a, to_b):
            to_a[...] = a[...]
            to_b[...] = b[...]

        return pl.pallas_call(
            hand_over,
            name="hand_over",
            out_shape=(
                jax.ShapeDtypeStruct((C, C, Z), f32),
                jax.ShapeDtypeStruct((3, C, C, Z), f32),
            ),
            in_specs=[vmem, vmem],
            out_specs=(vmem, vmem),
        )(level_out, velocity_out)

    field = P("gx", "gy", None)
    stack = P(None, "gx", "gy", None)
    return jax.shard_map(
        on_device,
        mesh=mesh,
        in_specs=(field, stack, P(None, None, "gx", "gy", None), field, field, field, P()),
        out_specs=(field, stack),
        check_vma=False,
    )
```

```python
import jax
import jax.numpy as jnp
from jax import lax
from jax.experimental import pallas as pl
from jax.experimental.pallas import tpu as pltpu
from jax.sharding import PartitionSpec as P

MESH = pl.DeviceIdType.MESH
BUOYANCY = 0.8
C = 16
Z = 128
ROW = (C, Z)
HALO = 24
PATCH = C + 3
U_COEF, U_FIRST, U_SECOND, U_WEIGHT, U_SPREAD, U_BUILD = 3, 6, 4, 2, 2, 7
ORDER = (
    "d02", "s02", "d00", "s00", "g02", "d01", "s01", "p02", "g00", "s03", "c02", "p00",
    "c00", "g01", "p01", "f02", "f00", "g03", "c01", "d12", "s12", "p03", "c03", "d10",
    "s10", "f01", "g12", "f03", "s13", "p12", "g10", "c12", "d11", "s11", "p10", "c10",
    "g13", "f12", "g11", "p13", "c13", "f10", "p11", "c11", "f13", "f11",
)

PARTNERS = (
    [(a, b) for a in (1, -1) for b in (1, -1)]
    + [(d, 0) for d in (3, -3, 1, -1)]
    + [(0, d) for d in (2, -2, 1, -1)]
)


def cubic_weights(position):
    squared = position * position
    cubed = squared * position
    return (
        (2.0 * squared - cubed - position) * 0.5,
        (3.0 * cubed - 5.0 * squared + 2.0) * 0.5,
        (4.0 * squared - 3.0 * cubed + position) * 0.5,
        (cubed - squared) * 0.5,
    )


def rolled(value, shift, axis):
    shift = shift % value.shape[axis]
    return value if shift == 0 else pltpu.roll(value, shift, axis)


def loop(low, high, body, carry, width):
    whole = (high - low) // width

    def several(n, carry):
        for k in range(width):
            carry = body(low + n * width + k, carry)
        return carry

    if whole > 1:
        carry = lax.fori_loop(0, whole, several, carry)
    else:
        whole = 0
    for i in range(low + whole * width, high):
        carry = body(i, carry)
    return carry


def make_kernel(count_x, count_y):
    def kernel(
        lev_any, vel_any, lab_any, frac_any, sx, sy, rates,
        out_l, out_v,
        frac, lab, ext, mid, coef, dif, lvl, weight,
        to_up, to_down, to_rim, own, from_down, from_up, from_rim,
        middle, tail_r, tail_l, got_tail_r, got_tail_l,
        far_r, far_l, near_r, near_l, got_far_r, got_far_l, got_near_r, got_near_l,
        send_sem, recv_sem, load_sem,
    ):
        me_x = lax.axis_index("gx")
        me_y = lax.axis_index("gy")

        def partner(dx, dy):
            return (lax.rem(me_x + dx + count_x, count_x), lax.rem(me_y + dy + count_y, count_y))

        barrier = pltpu.get_barrier_semaphore()
        for dx, dy in PARTNERS:
            pl.semaphore_signal(barrier, inc=1, device_id=partner(dx, dy), device_id_type=MESH)

        inner = ext.at[0, 0:3, 2 : C + 2, 0:C]
        loads = [
            pltpu.make_async_copy(src, dst, load_sem.at[n])
            for n, (src, dst) in enumerate(((lab_any, lab), (vel_any, inner), (frac_any, frac), (lev_any, lvl)))
        ]
        for load in loads:
            load.start()

        started = []

        def send(src, dst, dx, dy):
            index = len(started)
            copy = pltpu.make_async_remote_copy(
                src_ref=src, dst_ref=dst, send_sem=send_sem.at[index], recv_sem=recv_sem.at[index],
                device_id=partner(dx, dy), device_id_type=MESH,
            )
            copy.start()
            started.append(copy)
            return copy

        loads[0].wait()
        ext[0, 3, 2 : C + 2, 0:C, :] = jnp.where(lab[...] == 1, rates[1], rates[0])
        loads[1].wait()
        pl.semaphore_wait(barrier, len(PARTNERS))

        def send_halo(step, first, fields):
            e = ext.at[step]
            lo, hi = C, C + 2
            f = pl.ds(first, fields)
            copies = []
            for dx in (1, -1):
                for dy in (1, -1):
                    src_i, dst_i = (hi - 1, 1) if dx == 1 else (2, hi)
                    src_j, dst_j = (C - 1, HALO - 1) if dy == 1 else (0, C)
                    copies.append(
                        send(
                            e.at[f, src_i : src_i + 1, src_j : src_j + 1],
                            e.at[f, dst_i : dst_i + 1, dst_j : dst_j + 1],
                            dx, dy,
                        )
                    )
            copies += [
                send(e.at[f, lo:hi, 0:C], e.at[f, 0:2, 0:C], 1, 0),
                send(e.at[f, 2:4, 0:C], e.at[f, hi : hi + 2, 0:C], -1, 0),
                send(e.at[f, 2:hi, C - 2 : C], e.at[f, 2:hi, HALO - 2 : HALO], 0, 1),
                send(e.at[f, 2:hi, 0:2], e.at[f, 2:hi, C : C + 2], 0, -1),
            ]
            return copies

        def coefficients():
            def body(i, carry):
                rate = ext[0, 3, i]
                k = [
                    0.5 * (rate + ext[0, 3, i + 1]),
                    0.5 * (rate + ext[0, 3, i - 1]),
                    0.5 * (rate + rolled(rate, -1, 0)),
                    0.5 * (rate + rolled(rate, 1, 0)),
                    0.5 * (rate + rolled(rate, -1, 1)),
                    0.5 * (rate + rolled(rate, 1, 1)),
                ]
                coef[0, i] = 1.0 - ((k[0] + k[1]) + (k[2] + k[3]) + (k[4] + k[5]))
                for n in range(6):
                    coef[n + 1, i] = k[n]
                return carry

            loop(1, C + 3, body, 0, U_COEF)

        def swept(src, f, i, height):
            v = src[f, i]
            low = slice(0, height)
            total = coef[0, i, low] * v[low]
            total += coef[1, i, low] * src[f, i + 1, low]
            total += coef[2, i, low] * src[f, i - 1, low]
            total += coef[3, i, low] * rolled(v, -1, 0)[low]
            total += coef[4, i, low] * rolled(v, 1, 0)[low]
            total += coef[5, i, low] * rolled(v[low], -1, 1)
            total += coef[6, i, low] * rolled(v[low], 1, 1)
            return total

        def diffuse(step, f):
            def first(i, carry):
                mid[f, i] = swept(ext.at[step], f, i, HALO)
                return carry

            loop(1, C + 3, first, 0, U_FIRST)

            def second(i, carry):
                dif[f, i - 2] = swept(mid, f, i, C)
                return carry

            loop(2, C + 2, second, 0, U_SECOND)

        def weights(step):
            def body(x, carry):
                for n, value in enumerate(cubic_weights(frac[step, 2, x])):
                    weight[step, n, x] = value
                for axis in range(2):
                    base = frac[step, axis, x]
                    for c in range(4):
                        for n, value in enumerate(cubic_weights(rolled(base, c - 1, 1))):
                            weight[step, 4 + 16 * axis + 4 * c + n, x] = value
                return carry

            loop(0, C, body, 0, U_WEIGHT)

        line = lax.broadcasted_iota(jnp.int32, ROW, 0)

        def spread(step, f, slot):
            row_y = jnp.full(ROW, sy[step], jnp.int32)
            up = jnp.where(row_y == 1, 1.0, 0.0)
            stay = jnp.where(row_y == 0, 1.0, 0.0)
            down = jnp.where(row_y == -1, 1.0, 0.0)
            high = line < C // 2
            stay_h = jnp.where(high, stay, 0.0)
            stay_l = jnp.where(high, 0.0, stay)
            rim_own = jnp.where(high, down, up)
            rim_far = jnp.where(high, up, down)

            def emit(r, main, rim):
                to_up[slot, r] = main * up + rim * stay_h
                to_down[slot, r] = main * down + rim * stay_l
                own[slot, r] = main * stay + rim * rim_own
                to_rim[slot, r] = rim * rim_far

            def body(x, carry):
                if f < 3:
                    g = dif[f, x]
                else:
                    g = lvl[x] + BUOYANCY * dif[2, x]
                sums = [[None] * 4 for _ in range(4)]
                for c in range(4):
                    gc = rolled(g * weight[step, c, x], c - 1, 1)
                    for b in range(4):
                        h = gc * weight[step, 20 + 4 * c + b, x]
                        for a in range(4):
                            term = h * weight[step, 4 + 4 * c + a, x]
                            sums[a][b] = term if c == 0 else sums[a][b] + term
                mains, rims = [], []
                for a in range(4):
                    below = rolled(sums[a][0], -1, 0)
                    above = rolled(sums[a][2], 1, 0)
                    above2 = rolled(sums[a][3], 2, 0)
                    mains.append(
                        sums[a][1]
                        + jnp.where(line == C - 1, 0.0, below)
                        + jnp.where(line == 0, 0.0, above)
                        + jnp.where(line < 2, 0.0, above2)
                    )
                    rims.append(
                        jnp.where(line == C - 1, below, 0.0)
                        + jnp.where(line == 0, above, 0.0)
                        + jnp.where(line < 2, above2, 0.0)
                    )
                m0, m1, m2, r0, r1, r2 = carry
                emit(x, m0 + mains[0], r0 + rims[0])
                return (m1 + mains[1], m2 + mains[2], mains[3], r1 + rims[1], r2 + rims[2], rims[3])

            zero = jnp.zeros(ROW, jnp.float32)
            half = C // 2
            early, late = pl.ds(0, half), pl.ds(half, PATCH + 1 - half)
            carry = loop(0, half, body, (zero,) * 6, U_SPREAD)
            copies = [
                send(to_up.at[slot, early], from_down.at[slot, early], 0, 1),
                send(to_down.at[slot, early], from_up.at[slot, early], 0, -1),
            ]
            m0, m1, m2, r0, r1, r2 = loop(half, C, body, carry, U_SPREAD)
            emit(C, m0, r0)
            emit(C + 1, m1, r1)
            emit(C + 2, m2, r2)
            meta = jnp.full(ROW, sx[step], jnp.int32).astype(jnp.float32)
            to_up[slot, PATCH] = meta
            to_down[slot, PATCH] = meta
            to_rim[slot, PATCH] = meta
            own[slot, PATCH] = meta
            return copies + [
                send(to_up.at[slot, late], from_down.at[slot, late], 0, 1),
                send(to_down.at[slot, late], from_up.at[slot, late], 0, -1),
                send(to_rim.at[slot, :, 0:2], from_rim.at[slot, :, 0:2], 0, 2),
                send(to_rim.at[slot, :, C - 1 : C], from_rim.at[slot, :, C - 1 : C], 0, -2),
            ]

        sources = (own, from_down, from_up, from_rim)
        rim_lines = (line < 2) | (line == C - 1)

        def masks(slot, move):
            found = []
            wanted = jnp.full(ROW, move, jnp.int32).astype(jnp.float32)
            for n, source in enumerate(sources):
                hit = source[slot, PATCH] == wanted
                found.append(hit & rim_lines if n == 3 else hit)
            return found

        def gathered(slot, hits, r):
            total = None
            for hit, source in zip(hits, sources):
                part = jnp.where(hit, source[slot, r], 0.0)
                total = part if total is None else total + part
            return total

        def build(slot, move, store):
            hits = masks(slot, move)

            def body(q, carry):
                store(q, gathered(slot, hits, q + 1))
                return carry

            first, last = 0, C
            if move > -2:
                before = masks(slot, move - 1)
                for q in range(2):
                    store(q, gathered(slot, hits, q + 1) + gathered(slot, before, C + 1 + q))
                first = 2
            if move < 2:
                last = C - 1
            loop(first, last, body, 0, U_BUILD)
            if move < 2:
                store(C - 1, gathered(slot, hits, C) + gathered(slot, masks(slot, move + 1), 0))

        def transfer(slot, move, src, dst, dx):
            def store(q, value):
                src[slot, q] = value

            build(slot, move, store)
            return [send(src.at[slot], dst.at[slot], dx, 0)]

        def outer(slot):
            hits = masks(slot, 2)
            tail_r[slot, 0] = gathered(slot, hits, C + 1)
            tail_r[slot, 1] = gathered(slot, hits, C + 2)
            tail_l[slot, 0] = gathered(slot, masks(slot, -2), 0)
            tails = [
                send(tail_r.at[slot], got_tail_r.at[slot], 3, 0),
                send(tail_l.at[slot], got_tail_l.at[slot], -3, 0),
            ]
            right = transfer(slot, 2, far_r, got_far_r, 1)
            left = transfer(slot, -2, far_l, got_far_l, -1)
            return right, left, tails

        def prepare(slot):
            for move, ref in ((1, near_r), (-1, near_l), (0, middle)):
                def store(q, value):
                    ref[slot, q] = value

                build(slot, move, store)

        def pass_on(slot, near, got_far, got_near, dx, copies):
            wait_all(copies)
            near[slot] = near[slot] + got_far[slot]
            return [send(near.at[slot], got_near.at[slot], dx, 0)]

        def finish(slot, copies, store):
            wait_all(copies)
            for q in range(C):
                total = middle[slot, q] + (got_near_r[slot, q] + got_near_l[slot, q])
                if q < 2:
                    total = total + got_tail_r[slot, q]
                if q == C - 1:
                    total = total + got_tail_l[slot, 0]
                store(q, total)

        def target(step, f):
            def store(q, value):
                if step == 0 and f < 3:
                    ext[1, f, q + 2, 0:C] = value
                elif step == 0:
                    lvl[q] = value
                elif f < 3:
                    out_v[f, q] = value
                else:
                    out_l[q] = value

            return store

        def wait_all(copies):
            for copy in copies:
                copy.wait_recv()

        halo = {(0, f): [] for f in range(3)}
        halo[0, 2] = send_halo(0, 0, 4)
        loads[2].wait()
        loads[3].wait()
        weights(1)
        weights(0)
        state = {}

        def do_d(step, f):
            wait_all(halo[step, f])
            if (step, f) == (0, 2):
                coefficients()
            diffuse(step, f)

        def do_s(step, f):
            state[step, f] = spread(1 - step, f, 4 * step + f)

        def do_g(step, f):
            wait_all(state[step, f])
            state[step, f] = outer(4 * step + f)

        def do_c(step, f):
            right, left, rest = state[step, f]
            slot = 4 * step + f
            right = pass_on(slot, near_r, got_far_r, got_near_r, 1, right)
            left = pass_on(slot, near_l, got_far_l, got_near_l, -1, left)
            state[step, f] = right + left + rest

        def do_p(step, f):
            prepare(4 * step + f)

        def do_f(step, f):
            finish(4 * step + f, state[step, f], target(step, f))
            if step == 0 and f < 3:
                halo[1, f] = send_halo(1, f, 1)

        todo = {"d": do_d, "s": do_s, "g": do_g, "p": do_p, "c": do_c, "f": do_f}
        for word in ORDER:
            todo[word[0]](int(word[1]), int(word[2]))
        for copy in started:
            copy.wait_send()

    return kernel


def solution(mesh):
    count_x, count_y = mesh.shape["gx"], mesh.shape["gy"]
    copies = 8 + 3 * 8 + 2 * 4 * 12

    def on_device(level, velocity, fraction, shift_x, shift_y, labels, rates):
        vmem = pl.BlockSpec(memory_space=pltpu.VMEM)
        smem = pl.BlockSpec(memory_space=pltpu.SMEM)
        f32 = jnp.float32

        def rows(*lead):
            return pltpu.VMEM(lead + ROW, f32)

        level_out, velocity_out = pl.pallas_call(
            make_kernel(count_x, count_y),
            name="adjoint",
            out_shape=(
                jax.ShapeDtypeStruct((C, C, Z), f32),
                jax.ShapeDtypeStruct((3, C, C, Z), f32),
            ),
            in_specs=[pl.BlockSpec(memory_space=pl.ANY)] * 4 + [smem] * 3,
            out_specs=(vmem, vmem),
            scratch_shapes=[
                rows(2, 3, C),
                pltpu.VMEM((C, C, Z), jnp.int32),
                pltpu.VMEM((2, 4, C + 4, HALO, Z), f32),
                pltpu.VMEM((3, C + 4, HALO, Z), f32),
                pltpu.VMEM((7, C + 4, HALO, Z), f32),
                rows(3, C),
                rows(C),
                rows(2, 36, C),
                rows(8, PATCH + 1), rows(8, PATCH + 1), rows(8, PATCH + 1), rows(8, PATCH + 1),
                rows(8, PATCH + 1), rows(8, PATCH + 1), rows(8, PATCH + 1),
                rows(8, C), rows(8, 2), rows(8, 1), rows(8, 2), rows(8, 1),
                rows(8, C), rows(8, C), rows(8, C), rows(8, C), rows(8, C), rows(8, C), rows(8, C), rows(8, C),
                pltpu.SemaphoreType.DMA((copies,)),
                pltpu.SemaphoreType.DMA((copies,)),
                pltpu.SemaphoreType.DMA((4,)),
            ],
            compiler_params=pltpu.CompilerParams(
                collective_id=0, has_side_effects=True, vmem_limit_bytes=56 * 2**20
            ),
        )(level, velocity, labels, fraction, shift_x.reshape(2), shift_y.reshape(2), rates)

        def hand_over(a, b, to_a, to_b):
            to_a[...] = a[...]
            to_b[...] = b[...]

        return pl.pallas_call(
            hand_over,
            name="hand_over",
            out_shape=(
                jax.ShapeDtypeStruct((C, C, Z), f32),
                jax.ShapeDtypeStruct((3, C, C, Z), f32),
            ),
            in_specs=[vmem, vmem],
            out_specs=(vmem, vmem),
        )(level_out, velocity_out)

    field = P("gx", "gy", None)
    stack = P(None, "gx", "gy", None)
    return jax.shard_map(
        on_device,
        mesh=mesh,
        in_specs=(field, stack, P(None, None, "gx", "gy", None), field, field, field, P()),
        out_specs=(field, stack),
        check_vma=False,
    )
```
